32 devices in a mesh: groups: 2 (over y), row: 4 (over x, core), col: 4 (over z).
Axes of the slice: x: 2, y: 2, z: 4, core: 2. Of those that a mesh axis runs over, the one named last changes fastest.
Arguments:
- tokens: bfloat16 [8, 4, 16, 64, 768], P(('groups', 'row'), 'col'), parts along dimension 0, may hold values from -6 to 6
- assign: int32 [8, 4, 16, 1], P(('groups', 'row'), 'col'), parts along dimension 0, may hold values from 0 to 3; in each aligned block of 16 rows (0 to 15, 16 to 31, ..., all dimensions but the last counted through in order) at most 8 rows name the same one
- level_one: float32 [8, 768, 768], P(('groups', 'row'), 'col'), parts along dimension 0, may hold values from -6 to 6
- moment_one: float32 [8, 768, 768], P(('groups', 'row'), 'col'), parts along dimension 0, may hold values from -4 to 4
- level_two: float32 [8, 768, 768], P(('groups', 'col'), 'row'), parts along dimension 0, may hold values from -6 to 6
- moment_two: float32 [8, 768, 768], P(('groups', 'col'), 'row'), parts along dimension 0, may hold values from -4 to 4
- first_one: float32 [8, 4, 768, 768], P(('groups', 'row'), 'col'), parts along dimension 0, may hold values from -0.0014648438 to 0.0014648438
- second_one: float32 [8, 4, 768, 768], P(('groups', 'row'), 'col'), parts along dimension 0, may hold values from 1e-07 to 1e-06
- first_two: float32 [8, 4, 768, 768], P(('groups', 'row'), 'col'), parts along dimension 0, may hold values from -0.0014648438 to 0.0014648438
- second_two: float32 [8, 4, 768, 768], P(('groups', 'row'), 'col'), parts along dimension 0, may hold values from 1e-07 to 1e-06
Outputs:
- level_one_new: float32 [8, 768, 768], P(('groups', 'row'), 'col'), parts along dimension 0
- moment_one_new: float32 [8, 768, 768], P(('groups', 'row'), 'col'), parts along dimension 0
- level_two_new: float32 [8, 768, 768], P(('groups', 'col'), 'row'), parts along dimension 0
- moment_two_new: float32 [8, 768, 768], P(('groups', 'col'), 'row'), parts along dimension 0
The draws below stay inside these ranges and needn't reach their ends.
There are 2 independent parts, one for each index of `groups`. The reference program is written for one: setup_inputs(seed, part) draws one part's arguments, and reference() takes and returns one part's arrays. A program takes and returns all parts, laid end to end along the dimension named above; each array names one. Nothing has to cross between parts.
Inputs may be any that keep to these rules, and one draw needn't show every extreme that they name: `assign`: among the 16 blocks of one device, no level-1 module is named more than 8 times, and in some devices one is named exactly 8 times.
All inputs are finite; a program needn't handle non-finite values.
Results may differ from the reference program's by a relative error of at most 0.0012.
Values may be sent and summed in bfloat16 or wider, within the bound.
A program may use at most 128 MiB of HBM per device.

```python
import math
import jax
import jax.numpy as jnp
import numpy as np
from jax import lax

D = 768
BLK = 64
BLK_DEV = 16
LEVEL1 = 4
LEVEL2 = 4
CAP = 8


def steps_of(own_key, extent, split, low, top_value):
    def one(dim, blocks):
        draws = jax.random.uniform(jax.random.fold_in(jax.random.fold_in(own_key, 6), dim), (blocks,), jnp.float32, low / len(split), top_value / len(split))
        return jnp.repeat(jnp.exp(draws), extent[dim] // blocks).reshape((-1,) + (1,) * (len(extent) - dim - 1))

    level = one(*split[0])
    for cut in split[1:]:
        level = level * one(*cut)
    return level


def shared_out(key, own, number, rows, amount, top, reach, lean):
    order = jax.random.permutation(key, amount)
    crowded, common = portions_of(amount, rows * top, reach, lean, True), portions_of(amount, rows * top, reach, lean, False)
    places = jnp.arange(amount)

    def named(lengths, rotation):
        used = int((lengths > 0).sum())
        fixed = max(1, used // 4)
        moved = fixed + (places - fixed + rotation * (used - fixed)) % max(1, amount - fixed)
        return jnp.zeros((amount,), jnp.int32).at[order[jnp.where(places < fixed, places, moved)]].set(jnp.asarray(lengths, jnp.int32))

    lengths = jnp.where(number % 4 == 0, named(crowded, number // 4), named(common, number - number // 4 - 1))
    mixed = jax.random.permutation(jax.random.fold_in(own, 3), amount)
    donor, sink = mixed[0:amount // 2 * 2:2], mixed[1:amount // 2 * 2:2]
    slack = jnp.minimum(lengths[donor] - 1, reach - lengths[sink]) // 2
    slack = jnp.where((donor == order[0]) | (sink == order[0]) | (lengths[sink] == 0), 0, jnp.maximum(slack, 0))
    moved = jax.random.randint(jax.random.fold_in(own, 4), (amount // 2,), 0, 1 << 20) % (slack + 1)
    lengths = lengths.at[donor].add(-moved).at[sink].add(moved)
    members = jnp.searchsorted(jnp.cumsum(lengths), jnp.arange(rows * top), side="right").astype(jnp.int32)
    table = members.reshape(top, rows).T
    table = table[jax.random.permutation(jax.random.fold_in(own, 1), rows)]
    rotation = jax.random.randint(jax.random.fold_in(own, 2), (rows, 1), 0, top)
    return jnp.take_along_axis(table, (jnp.arange(top)[None, :] + rotation) % top, axis=1)


def portions_of(count, total, reach, lean, full):
    weights = [(1 << 20) // math.isqrt(rank ** lean) + 1 for rank in range(1, count + 1)]
    largest = reach if full else min(reach, max(-(-total // count), total * weights[0] // sum(weights)))
    least = 1 if total - largest >= count - 1 else 0
    counts, surplus = [largest] + [least] * (count - 1), total - largest - least * (count - 1)
    while surplus > 0:
        movable = [i for i in range(1, count) if counts[i] < largest] or [i for i in range(1, count) if counts[i] < reach]
        mass, left = sum([weights[i] for i in movable]), surplus
        for i in movable:
            more = min(reach - counts[i], max(1, left * weights[i] // mass), surplus)
            counts[i] = counts[i] + more
            surplus = surplus - more
    return np.array(counts)


def normal_values(key, extent, spread, most, cuts=(), held_as=jnp.bfloat16):
    array = spread * jax.random.normal(key, extent, jnp.float32)
    if cuts:
        array = array * steps_of(key, extent, cuts, -0.22, 0.18)
    return jnp.clip(array, -most, most).astype(held_as)


def setup_inputs(seed: int = 0, part: int = 0) -> dict:
    splits = jax.random.split(jax.random.key(seed), 11)
    part_keys = jax.random.split(jax.random.fold_in(splits[10], part), 11)
    tokens = normal_values(part_keys[0], (LEVEL1, LEVEL2, BLK_DEV, BLK, D), 1.0, 6.0, ((0, 4), (1, 4)))
    assign_keys = jax.random.split(jax.random.fold_in(part_keys[1], 1), LEVEL1 * LEVEL2 * BLK_DEV // BLK_DEV)
    assign_turns = jax.random.permutation(jax.random.fold_in(part_keys[1], 3), LEVEL1 * LEVEL2 * BLK_DEV // BLK_DEV)
    assign = jax.vmap(lambda own, number: shared_out(jax.random.fold_in(part_keys[1], 2), own, number, BLK_DEV, LEVEL1, 1, CAP, 2))(assign_keys, assign_turns).reshape((LEVEL1, LEVEL2, BLK_DEV, 1))
    level_one = normal_values(part_keys[2], (LEVEL1, D, D), 1.0, 6.0, ((0, 4), (1, 4)), jnp.float32)
    moment_one = normal_values(part_keys[3], (LEVEL1, D, D), 0.3, 4.0, ((0, 4), (1, 4)), jnp.float32)
    level_two = normal_values(part_keys[4], (LEVEL2, D, D), 1.0, 6.0, ((0, 4), (1, 4)), jnp.float32)
    moment_two = normal_values(part_keys[5], (LEVEL2, D, D), 0.3, 4.0, ((0, 4), (1, 4)), jnp.float32)
    first_one = normal_values(part_keys[6], (LEVEL1, LEVEL2, D, D), 0.0001, 0.0014648438, ((0, 4), (1, 4)), jnp.float32)
    second_one = jnp.clip(jnp.exp(math.log(9.999999974752427e-07) - 2.3025851 * jax.random.uniform(part_keys[7], (LEVEL1, LEVEL2, D, D), jnp.float32) ** steps_of(part_keys[7], (LEVEL1, LEVEL2, D, D), ((0, 4), (1, 4)), -0.2, 0.2)), 1.0000000116860974e-07, 9.999999974752427e-07)
    first_two = normal_values(part_keys[8], (LEVEL1, LEVEL2, D, D), 0.0001, 0.0014648438, ((0, 4), (1, 4)), jnp.float32)
    second_two = jnp.clip(jnp.exp(math.log(9.999999974752427e-07) - 2.3025851 * jax.random.uniform(part_keys[9], (LEVEL1, LEVEL2, D, D), jnp.float32) ** steps_of(part_keys[9], (LEVEL1, LEVEL2, D, D), ((0, 4), (1, 4)), -0.2, 0.2)), 1.0000000116860974e-07, 9.999999974752427e-07)
    return dict(tokens=tokens, assign=assign, level_one=level_one, moment_one=moment_one, level_two=level_two, moment_two=moment_two, first_one=first_one, second_one=second_one, first_two=first_two, second_two=second_two)


norm_eps = 1e-06
adam_eps = 1e-08
beta_first = 0.9
beta_second = 0.95
bias_first = 0.19
bias_second = 0.0975
inner_rate = 0.3
decay_rate = 0.1
outer_rate = 0.7
momentum = 0.9

def block_slots(destination, levels, capacity):
    number = destination.shape[0]
    position = jnp.arange(number, dtype=jnp.int32)
    earlier = (destination[:, None] == destination[None, :]) & (position[None, :] < position[:, None])
    ranking = lax.optimization_barrier(jnp.sum(earlier.astype(jnp.int32), axis=1))
    target_slot = destination * capacity + ranking
    every_slot = jnp.arange(levels * capacity, dtype=jnp.int32)
    return (every_slot[:, None] == target_slot[None, :]).astype(jnp.bfloat16)

def route_blocks(blocks, destination, levels, capacity):
    select = block_slots(destination, levels, capacity)
    number, length, features = blocks.shape
    packed = jnp.dot(select, blocks.reshape(number, length * features), preferred_element_type=jnp.float32)
    packed = packed.astype(jnp.bfloat16).reshape(levels, capacity, length, features)
    filled = lax.optimization_barrier(jnp.sum(select, axis=1)).reshape(levels, capacity)
    return (packed, filled)

def normalized(hidden):
    factor = lax.rsqrt(lax.optimization_barrier(jnp.mean(hidden * hidden, axis=-1, keepdims=True)) + norm_eps)
    return (hidden * factor, factor)

def silu_slope(preact, gating):
    return gating * (1.0 + preact * (1.0 - gating))

def path_gradients(path_slots, filled, first_weight, second_weight, loss_scale):
    number, length, features = path_slots.shape
    inputs = path_slots.astype(jnp.float32)
    targets = jnp.concatenate([inputs[:, 1:], jnp.zeros((number, 1, features), jnp.float32)], axis=1)
    position = jnp.arange(length, dtype=jnp.int32)
    loss_weight = filled.astype(jnp.float32)[:, None] * (position < length - 1).astype(jnp.float32)[None, :] * loss_scale
    inputs = inputs.reshape(number * length, features)
    targets = targets.reshape(number * length, features)
    loss_weight = loss_weight.reshape(number * length, 1)
    shrink = features ** (-0.5)
    normed_one, factor_one = normalized(inputs)
    act_one = normed_one.astype(jnp.bfloat16)
    pre_one = shrink * jnp.dot(act_one, first_weight, preferred_element_type=jnp.float32)
    gate_one = jax.nn.sigmoid(pre_one)
    hidden = inputs + pre_one * gate_one
    normed_two, factor_two = normalized(hidden)
    act_two = normed_two.astype(jnp.bfloat16)
    pre_two = shrink * jnp.dot(act_two, second_weight, preferred_element_type=jnp.float32)
    gate_two = jax.nn.sigmoid(pre_two)
    output = hidden + pre_two * gate_two
    grad_out = loss_weight * (output - targets)
    grad_pre_two = (grad_out * silu_slope(pre_two, gate_two)).astype(jnp.bfloat16)
    grad_second = shrink * lax.dot_general(act_two, grad_pre_two, (((0,), (0,)), ((), ())), preferred_element_type=jnp.float32)
    grad_act_two = shrink * lax.dot_general(grad_pre_two, second_weight, (((1,), (1,)), ((), ())), preferred_element_type=jnp.float32)
    grad_hidden = grad_out + factor_two * (grad_act_two - normed_two * lax.optimization_barrier(jnp.mean(grad_act_two * normed_two, axis=-1, keepdims=True)))
    grad_pre_one = (grad_hidden * silu_slope(pre_one, gate_one)).astype(jnp.bfloat16)
    grad_first = shrink * lax.dot_general(act_one, grad_pre_one, (((0,), (0,)), ((), ())), preferred_element_type=jnp.float32)
    return (grad_first, grad_second)

def adam_direction(gradient, first_moment, second_moment):
    first_new = beta_first * first_moment + (1.0 - beta_first) * gradient
    second_new = beta_second * second_moment + (1.0 - beta_second) * gradient * gradient
    return first_new / bias_first / (jnp.sqrt(second_new / bias_second) + adam_eps)

def outer_update(weight, moment, mean_direction):
    pseudo = inner_rate * (mean_direction + decay_rate * weight)
    moment_new = momentum * moment + pseudo
    return (weight - outer_rate * (pseudo + momentum * moment_new), moment_new)

def reference(tokens, assign, level_one, moment_one, level_two, moment_two, first_one, second_one, first_two, second_two):
    capacity = CAP
    loss_scale = 1.0 / (BLK_DEV * BLK)

    def route_device(blocks, chosen):
        return route_blocks(blocks, chosen[:, 0], LEVEL1, capacity)
    packed, filled = jax.vmap(jax.vmap(route_device))(tokens, assign)

    def one_path(path_index):
        row_index = path_index // LEVEL2
        col_index = path_index % LEVEL2
        column_packed = lax.dynamic_index_in_dim(packed, col_index, 1, keepdims=False)
        path_slots = lax.dynamic_index_in_dim(column_packed, row_index, 1, keepdims=False)
        column_filled = lax.dynamic_index_in_dim(filled, col_index, 1, keepdims=False)
        path_filled = lax.dynamic_index_in_dim(column_filled, row_index, 1, keepdims=False)
        path_slots = path_slots.reshape(LEVEL1 * capacity, BLK, D)
        path_filled = path_filled.reshape(LEVEL1 * capacity)
        first_weight = lax.dynamic_index_in_dim(level_one, row_index, 0, keepdims=False).astype(jnp.bfloat16)
        second_weight = lax.dynamic_index_in_dim(level_two, col_index, 0, keepdims=False).astype(jnp.bfloat16)
        grad_first, grad_second = path_gradients(path_slots, path_filled, first_weight, second_weight, loss_scale)

        def pick(states):
            return lax.dynamic_index_in_dim(lax.dynamic_index_in_dim(states, row_index, 0, keepdims=False), col_index, 0, keepdims=False)
        direction_one = adam_direction(grad_first, pick(first_one), pick(second_one))
        direction_two = adam_direction(grad_second, pick(first_two), pick(second_two))
        return (direction_one, direction_two)
    direction_one, direction_two = lax.map(one_path, jnp.arange(LEVEL1 * LEVEL2, dtype=jnp.int32))
    direction_one = direction_one.reshape(LEVEL1, LEVEL2, D, D)
    direction_two = direction_two.reshape(LEVEL1, LEVEL2, D, D)
    mean_one = lax.optimization_barrier(jnp.sum(direction_one, axis=1)) / LEVEL2
    mean_two = lax.optimization_barrier(jnp.sum(direction_two, axis=0)) / LEVEL1
    level_one_new, moment_one_new = outer_update(level_one, moment_one, mean_one)
    level_two_new, moment_two_new = outer_update(level_two, moment_two, mean_two)
    return (level_one_new, moment_one_new, level_two_new, moment_two_new)
```

```python
import functools

import jax
import jax.numpy as jnp
from jax import lax
from jax.experimental import pallas as pl
from jax.experimental.pallas import tpu as pltpu
from jax.sharding import PartitionSpec as P

norm_eps = 1e-06
adam_eps = 1e-08
beta_first = 0.9
beta_second = 0.95
bias_first = 0.19
bias_second = 0.0975
inner_rate = 0.3
decay_rate = 0.1
outer_rate = 0.7
momentum = 0.9

tile_slots = 4
MESH = pl.DeviceIdType.MESH


def flipped(index, mask):
    bit = 1
    while bit <= mask:
        if mask & bit:
            index = index + bit * (1 - 2 * (lax.div(index, bit) % 2))
        bit *= 2
    return index


def outer_update(weight, moment, mean_direction):
    pseudo = inner_rate * (mean_direction + decay_rate * weight)
    moment_new = momentum * moment + pseudo
    return weight - outer_rate * (pseudo + momentum * moment_new), moment_new


def adam_direction(gradient, first_moment, second_moment):
    first_new = beta_first * first_moment + (1.0 - beta_first) * gradient
    second_new = beta_second * second_moment + (1.0 - beta_second) * gradient * gradient
    return (first_new * (1.0 / bias_first)) / (
        jnp.sqrt(second_new * (1.0 / bias_second)) + adam_eps
    )


def kernel(
    levels, columns, capacity,
    assign_ref, tokens_ref, level_one_ref, moment_one_ref, level_two_ref, moment_two_ref,
    first_one_ref, second_one_ref, first_two_ref, second_two_ref,
    new_one_ref, new_moment_one_ref, new_two_ref, new_moment_two_ref,
    packed, arrived, count_out, count_in, weight_one, weight_two,
    adam_one_m, adam_one_v, adam_two_m, adam_two_v, grad_one, grad_two,
    own_one, own_two, out_one, out_two, in_one, in_two,
    local_sem, piece_send, piece_recv, count_send, count_recv,
    w1_send, w1_recv, w2_send, w2_forward, w2_recv, d1_send, d1_recv, d2_send, d2_recv,
):
    row = lax.axis_index("row")
    col = lax.axis_index("col")
    number, length, features = tokens_ref.shape
    rows_one = features // columns
    rows_two = features // levels
    piece = min(capacity, tile_slots)
    own_pieces = capacity // piece
    per_tile = tile_slots // piece
    tiles = levels * capacity // tile_slots
    tile_rows = tile_slots * length
    shrink = features ** (-0.5)
    loss_scale = 1.0 / (number * length)

    barrier = pltpu.get_barrier_semaphore()
    for o in range(1, levels):
        pl.semaphore_signal(
            barrier, inc=1, device_id={"row": flipped(row, o)}, device_id_type=MESH
        )
    for o in range(1, columns):
        pl.semaphore_signal(
            barrier, inc=1, device_id={"col": (col + o) % columns}, device_id_type=MESH
        )

    loads = [
        pltpu.make_async_copy(source, target, local_sem.at[i])
        for i, (source, target) in enumerate((
            (first_one_ref, adam_one_m), (second_one_ref, adam_one_v),
            (first_two_ref, adam_two_m), (second_two_ref, adam_two_v),
        ))
    ]
    for load in loads:
        load.start()

    def shard_one(index):
        return weight_one.at[pl.ds(pl.multiple_of(index * rows_one, rows_one), rows_one)]

    def shard_two(index):
        return weight_two.at[pl.ds(pl.multiple_of(index * rows_two, rows_two), rows_two)]

    shard_one(col)[...] = level_one_ref[...].astype(jnp.bfloat16)
    shard_two(row)[...] = level_two_ref[...].astype(jnp.bfloat16)

    pl.semaphore_wait(barrier, levels - 1 + columns - 1)

    def send_one(o):
        return pltpu.make_async_remote_copy(
            src_ref=shard_one(col), dst_ref=shard_one(col),
            send_sem=w1_send.at[o], recv_sem=w1_recv.at[o],
            device_id={"col": (col + o) % columns}, device_id_type=MESH,
        )

    def send_two(o):
        return pltpu.make_async_remote_copy(
            src_ref=shard_two(row), dst_ref=shard_two(row),
            send_sem=w2_send.at[o], recv_sem=w2_recv.at[o],
            device_id={"row": flipped(row, o)}, device_id_type=MESH,
        )

    def forward_two(o):
        source = flipped(row, o)
        return pltpu.make_async_remote_copy(
            src_ref=shard_two(source), dst_ref=shard_two(source),
            send_sem=w2_forward.at[o], recv_sem=w2_recv.at[o + 1],
            device_id={"row": flipped(row, 1)}, device_id_type=MESH,
        )

    direct_two = [o for o in range(1, levels) if o == 1 or o % 2 == 0]
    for o in range(1, columns):
        send_one(o).start()
    for o in reversed(direct_two):
        send_two(o).start()

    def send_piece(o, p):
        start = (o - 1) * capacity + p * piece
        return pltpu.make_async_remote_copy(
            src_ref=packed.at[pl.ds(start * length, piece * length)],
            dst_ref=arrived.at[pl.ds((start + capacity) * length, piece * length)],
            send_sem=piece_send.at[o * own_pieces + p],
            recv_sem=piece_recv.at[o * own_pieces + p],
            device_id={"row": flipped(row, o)}, device_id_type=MESH,
        )

    def send_count(o):
        return pltpu.make_async_remote_copy(
            src_ref=count_out.at[o], dst_ref=count_in.at[o],
            send_sem=count_send.at[o], recv_sem=count_recv.at[o],
            device_id={"row": flipped(row, o)}, device_id_type=MESH,
        )

    for o in list(range(2, levels)) + [1, 0]:
        target = flipped(row, o)
        word = jnp.int32(0)
        scale = jnp.int32(1)
        count = jnp.int32(0)
        for b in range(number):
            hit = assign_ref[b] == target
            word = word + jnp.where(hit, b * scale, 0)
            scale = jnp.where(hit, scale * 16, scale)
            count = count + jnp.where(hit, 1, 0)
        if o == 0:
            count_in[0] = jnp.full((8, 128), count, jnp.int32)
        else:
            count_out[o] = jnp.full((8, 128), count, jnp.int32)
            send_count(o).start()
        for k in range(capacity):
            block = lax.shift_right_logical(word, jnp.int32(4 * k)) & 15
            value = tokens_ref[block]
            value = jnp.where(k < count, value, jnp.zeros_like(value))
            if o == 0:
                arrived[pl.ds(k * length, length)] = value
            else:
                packed[pl.ds(((o - 1) * capacity + k) * length, length)] = value
                if (k + 1) % piece == 0:
                    send_piece(o, k // piece).start()

    for o in range(2, levels, 2):
        send_two(o).wait_recv()
        forward_two(o).start()

    grad_one[...] = jnp.zeros_like(grad_one)
    grad_two[...] = jnp.zeros_like(grad_two)
    for o in range(1, levels):
        send_count(o).wait_recv()
    for o in range(1, columns):
        send_one(o).wait_recv()
    for o in range(1, levels, 2):
        send_two(o).wait_recv()

    def tile_body(t, carry):
        for i in range(per_tile):
            g = t * per_tile + i
            part = arrived.at[pl.ds(pl.multiple_of(g * piece * length, piece * length), piece * length)]

            @pl.when(g >= own_pieces)
            def _():
                pltpu.make_async_remote_copy(
                    src_ref=part, dst_ref=part,
                    send_sem=piece_send.at[g], recv_sem=piece_recv.at[g],
                    device_id={"row": flipped(row, 1)}, device_id_type=MESH,
                ).wait_recv()

        inputs = arrived[pl.ds(pl.multiple_of(t * tile_rows, tile_rows), tile_rows)].astype(jnp.float32)
        place = lax.broadcasted_iota(jnp.int32, (tile_rows, 1), 0)
        inner = place % length
        slot = t * tile_slots + place // length
        if capacity >= tile_slots:
            count = count_in[(t * tile_slots) // capacity][0:1, 0:1]
        else:
            count = jnp.zeros((1, 1), jnp.int32)
            per_source = tile_slots // capacity
            for i in range(per_source):
                own = count_in[t * per_source + i][0:1, 0:1]
                count = jnp.where(place // (capacity * length) == i, own, count)
        filled = (slot % capacity < count).astype(jnp.float32)
        loss_weight = filled * (inner < length - 1).astype(jnp.float32) * loss_scale
        targets = jnp.where(inner < length - 1, pltpu.roll(inputs, tile_rows - 1, 0), 0.0)

        factor_one = lax.rsqrt(jnp.mean(inputs * inputs, axis=-1, keepdims=True) + norm_eps)
        act_one = (inputs * factor_one).astype(jnp.bfloat16)
        pre_one = shrink * jnp.dot(act_one, weight_one[...], preferred_element_type=jnp.float32)
        gate_one = jax.nn.sigmoid(pre_one)
        hidden = inputs + pre_one * gate_one
        factor_two = lax.rsqrt(jnp.mean(hidden * hidden, axis=-1, keepdims=True) + norm_eps)
        normed_two = hidden * factor_two
        act_two = normed_two.astype(jnp.bfloat16)
        pre_two = shrink * jnp.dot(act_two, weight_two[...], preferred_element_type=jnp.float32)
        gate_two = jax.nn.sigmoid(pre_two)
        grad_out = loss_weight * (hidden + pre_two * gate_two - targets)
        grad_pre_two = (grad_out * (gate_two * (1.0 + pre_two * (1.0 - gate_two)))).astype(jnp.bfloat16)
        grad_two[...] += lax.dot_general(
            act_two, grad_pre_two, (((0,), (0,)), ((), ())), preferred_element_type=jnp.float32
        )
        grad_act = shrink * lax.dot_general(
            grad_pre_two, weight_two[...], (((1,), (1,)), ((), ())),
            preferred_element_type=jnp.float32,
        )
        grad_hidden = grad_out + factor_two * (
            grad_act - normed_two * jnp.mean(grad_act * normed_two, axis=-1, keepdims=True)
        )
        grad_pre_one = (grad_hidden * (gate_one * (1.0 + pre_one * (1.0 - gate_one)))).astype(jnp.bfloat16)
        grad_one[...] += lax.dot_general(
            act_one, grad_pre_one, (((0,), (0,)), ((), ())), preferred_element_type=jnp.float32
        )
        return carry

    lax.fori_loop(0, tiles, tile_body, 0)

    for load in loads:
        load.wait()

    def direction(grad, first, second, index, rows):
        at = pl.ds(pl.multiple_of(index * rows, rows), rows)
        return adam_direction(shrink * grad[at, :], first[at, :], second[at, :])

    def send_direction_one(o):
        return pltpu.make_async_remote_copy(
            src_ref=out_one.at[o], dst_ref=in_one.at[o],
            send_sem=d1_send.at[o], recv_sem=d1_recv.at[o],
            device_id={"col": (col + o) % columns}, device_id_type=MESH,
        )

    def send_direction_two(o):
        return pltpu.make_async_remote_copy(
            src_ref=out_two.at[o], dst_ref=in_two.at[o],
            send_sem=d2_send.at[o], recv_sem=d2_recv.at[o],
            device_id={"row": flipped(row, o)}, device_id_type=MESH,
        )

    for o in range(1, max(levels, columns)):
        if o < columns:
            out_one[o] = direction(
                grad_one, adam_one_m, adam_one_v, (col + o) % columns, rows_one
            ).astype(jnp.bfloat16)
            send_direction_one(o).start()
        if o < levels:
            q = levels - o
            out_two[q] = direction(
                grad_two, adam_two_m, adam_two_v, flipped(row, q), rows_two
            ).astype(jnp.bfloat16)
            send_direction_two(q).start()
    own_one[...] = direction(grad_one, adam_one_m, adam_one_v, col, rows_one)
    own_two[...] = direction(grad_two, adam_two_m, adam_two_v, row, rows_two)

    for o in range(1, levels):
        send_direction_two(o).wait_recv()
    total_two = own_two[...]
    for o in range(1, levels):
        total_two = total_two + in_two[o].astype(jnp.float32)
    new, moment = outer_update(level_two_ref[...], moment_two_ref[...], total_two / levels)
    new_two_ref[...] = new
    new_moment_two_ref[...] = moment

    for o in range(1, columns):
        send_direction_one(o).wait_recv()
    total_one = own_one[...]
    for o in range(1, columns):
        total_one = total_one + in_one[o].astype(jnp.float32)
    new, moment = outer_update(level_one_ref[...], moment_one_ref[...], total_one / columns)
    new_one_ref[...] = new
    new_moment_one_ref[...] = moment

    for o in range(1, columns):
        send_one(o).wait_send()
        send_direction_one(o).wait_send()
    for o in direct_two:
        send_two(o).wait_send()
    for o in range(2, levels, 2):
        forward_two(o).wait_send()
    for o in range(1, levels):
        send_count(o).wait_send()
        send_direction_two(o).wait_send()
        for p in range(own_pieces):
            send_piece(o, p).wait_send()


def per_device(
    tokens, assign, level_one, moment_one, level_two, moment_two,
    first_one, second_one, first_two, second_two,
):
    levels = lax.axis_size("row")
    columns = lax.axis_size("col")
    blocks = tokens[0, 0]
    number, length, features = blocks.shape
    capacity = max(2, (2 * number + levels - 1) // levels)
    rows_one = features // columns
    rows_two = features // levels
    piece = min(capacity, tile_slots)
    pieces = levels * capacity // piece
    f32, bf16 = jnp.float32, jnp.bfloat16
    vmem = pl.BlockSpec(memory_space=pltpu.VMEM)
    smem = pl.BlockSpec(memory_space=pltpu.SMEM)
    hbm = pl.BlockSpec(memory_space=pl.ANY)
    dma = pltpu.SemaphoreType.DMA
    square = (features, features)
    outs = pl.pallas_call(
        functools.partial(kernel, levels, columns, capacity),
        out_shape=[
            jax.ShapeDtypeStruct((rows_one, features), f32),
            jax.ShapeDtypeStruct((rows_one, features), f32),
            jax.ShapeDtypeStruct((rows_two, features), f32),
            jax.ShapeDtypeStruct((rows_two, features), f32),
        ],
        in_specs=[smem] + [vmem] * 5 + [hbm] * 4,
        out_specs=[vmem] * 4,
        scratch_shapes=[
            pltpu.VMEM(((levels - 1) * capacity * length, features), bf16),
            pltpu.VMEM((levels * capacity * length, features), bf16),
            pltpu.VMEM((levels, 8, 128), jnp.int32),
            pltpu.VMEM((levels, 8, 128), jnp.int32),
            pltpu.VMEM(square, bf16),
            pltpu.VMEM(square, bf16),
            pltpu.VMEM(square, f32),
            pltpu.VMEM(square, f32),
            pltpu.VMEM(square, f32),
            pltpu.VMEM(square, f32),
            pltpu.VMEM(square, f32),
            pltpu.VMEM(square, f32),
            pltpu.VMEM((rows_one, features), f32),
            pltpu.VMEM((rows_two, features), f32),
            pltpu.VMEM((columns, rows_one, features), bf16),
            pltpu.VMEM((levels, rows_two, features), bf16),
            pltpu.VMEM((columns, rows_one, features), bf16),
            pltpu.VMEM((levels, rows_two, features), bf16),
            dma((4,)),
            dma((pieces,)), dma((pieces,)),
            dma((levels,)), dma((levels,)),
            dma((columns,)), dma((columns,)),
            dma((levels,)), dma((levels,)), dma((levels,)),
            dma((columns,)), dma((columns,)),
            dma((levels,)), dma((levels,)),
        ],
        compiler_params=pltpu.CompilerParams(
            collective_id=0, has_side_effects=True, vmem_limit_bytes=56 * 1024 * 1024
        ),
        name="outer_round",
    )(
        assign.reshape(number), blocks, level_one[0], moment_one[0], level_two[0], moment_two[0],
        first_one[0, 0], second_one[0, 0], first_two[0, 0], second_two[0, 0],
    )
    return tuple(out[None] for out in outs)


def solution(mesh):
    in_specs = (
        P(("groups", "row"), "col", None, None, None),
        P(("groups", "row"), "col", None, None),
        P(("groups", "row"), "col", None),
        P(("groups", "row"), "col", None),
        P(("groups", "col"), "row", None),
        P(("groups", "col"), "row", None),
        P(("groups", "row"), "col", None, None),
        P(("groups", "row"), "col", None, None),
        P(("groups", "row"), "col", None, None),
        P(("groups", "row"), "col", None, None),
    )
    out_specs = (
        P(("groups", "row"), "col", None),
        P(("groups", "row"), "col", None),
        P(("groups", "col"), "row", None),
        P(("groups", "col"), "row", None),
    )
    return jax.shard_map(
        per_device, mesh=mesh, in_specs=in_specs, out_specs=out_specs, check_vma=False
    )
```

```python
import functools

import jax
import jax.numpy as jnp
from jax import lax
from jax.experimental import pallas as pl
from jax.experimental.pallas import tpu as pltpu
from jax.sharding import PartitionSpec as P

norm_eps = 1e-06
adam_eps = 1e-08
beta_first = 0.9
beta_second = 0.95
bias_first = 0.19
bias_second = 0.0975
inner_rate = 0.3
decay_rate = 0.1
outer_rate = 0.7
momentum = 0.9

tile_slots = 4
MESH = pl.DeviceIdType.MESH


def flipped(index, mask):
    bit = 1
    while bit <= mask:
        if mask & bit:
            index = index + bit * (1 - 2 * (lax.div(index, bit) % 2))
        bit *= 2
    return index


def outer_update(weight, moment, mean_direction):
    pseudo = inner_rate * (mean_direction + decay_rate * weight)
    moment_new = momentum * moment + pseudo
    return weight - outer_rate * (pseudo + momentum * moment_new), moment_new


def adam_direction(gradient, first_moment, second_moment):
    first_new = beta_first * first_moment + (1.0 - beta_first) * gradient
    second_new = beta_second * second_moment + (1.0 - beta_second) * gradient * gradient
    return (first_new * (1.0 / bias_first)) / (
        jnp.sqrt(second_new * (1.0 / bias_second)) + adam_eps
    )


def kernel(
    levels, columns, capacity,
    assign_ref, tokens_hbm, level_one_hbm, level_two_hbm,
    first_one_ref, second_one_ref, first_two_ref, second_two_ref,
    mean_one_ref, mean_two_ref,
    tokens_ref, level_one_ref, level_two_ref, relay_in, relay_out, packed, arrived, count_out, count_in, weight_one, weight_two,
    adam_one_m, adam_one_v, adam_two_m, adam_two_v, grad_one, grad_two,
    own_one, own_two, out_one, out_two, in_one, in_two,
    local_sem, piece_send, piece_recv, count_send, count_recv,
    w1_send, w1_recv, w2_send, w2_forward, w2_recv, d1_send, d1_recv, d2_send, d2_recv,
    relay_send, relay_recv,
):
    row = lax.axis_index("row")
    col = lax.axis_index("col")
    number, length, features = tokens_ref.shape
    rows_one = features // columns
    rows_two = features // levels
    piece = min(capacity, tile_slots)
    own_pieces = capacity // piece
    per_tile = tile_slots // piece
    tiles = levels * capacity // tile_slots
    tile_rows = tile_slots * length
    shrink = features ** (-0.5)
    loss_scale = 1.0 / (number * length)

    barrier = pltpu.get_barrier_semaphore()
    for o in range(1, levels):
        pl.semaphore_signal(
            barrier, inc=1, device_id={"row": flipped(row, o)}, device_id_type=MESH
        )
    for o in range(1, columns):
        pl.semaphore_signal(
            barrier, inc=1, device_id={"col": (col + o) % columns}, device_id_type=MESH
        )

    loads = [
        pltpu.make_async_copy(source, target, local_sem.at[i])
        for i, (source, target) in enumerate((
            (first_one_ref, adam_one_m), (second_one_ref, adam_one_v),
            (first_two_ref, adam_two_m), (second_two_ref, adam_two_v),
        ))
    ]
    inputs_in = [
        pltpu.make_async_copy(source, target, local_sem.at[4 + i])
        for i, (source, target) in enumerate((
            (level_two_hbm, level_two_ref), (tokens_hbm, tokens_ref), (level_one_hbm, level_one_ref),
        ))
    ]
    for load in inputs_in:
        load.start()

    def shard_one(index):
        return weight_one.at[pl.ds(pl.multiple_of(index * rows_one, rows_one), rows_one)]

    def shard_two(index):
        return weight_two.at[pl.ds(pl.multiple_of(index * rows_two, rows_two), rows_two)]

    def send_one(o):
        return pltpu.make_async_remote_copy(
            src_ref=shard_one(col), dst_ref=shard_one(col),
            send_sem=w1_send.at[o], recv_sem=w1_recv.at[o],
            device_id={"col": (col + o) % columns}, device_id_type=MESH,
        )

    def send_two(o):
        return pltpu.make_async_remote_copy(
            src_ref=shard_two(row), dst_ref=shard_two(row),
            send_sem=w2_send.at[o], recv_sem=w2_recv.at[o],
            device_id={"row": flipped(row, o)}, device_id_type=MESH,
        )

    def forward_two(o):
        source = flipped(row, o)
        return pltpu.make_async_remote_copy(
            src_ref=shard_two(source), dst_ref=shard_two(source),
            send_sem=w2_forward.at[o], recv_sem=w2_recv.at[o + 1],
            device_id={"row": flipped(row, 1)}, device_id_type=MESH,
        )

    direct_two = [o for o in range(1, levels) if o == 1 or o % 2 == 0]
    def send_piece(o, p):
        start = (o - 1) * capacity + p * piece
        return pltpu.make_async_remote_copy(
            src_ref=packed.at[pl.ds(start * length, piece * length)],
            dst_ref=arrived.at[pl.ds((start + capacity) * length, piece * length)],
            send_sem=piece_send.at[o * own_pieces + p],
            recv_sem=piece_recv.at[o * own_pieces + p],
            device_id={"row": flipped(row, o)}, device_id_type=MESH,
        )

    def send_count(o):
        return pltpu.make_async_remote_copy(
            src_ref=count_out.at[o], dst_ref=count_in.at[o],
            send_sem=count_send.at[o], recv_sem=count_recv.at[o],
            device_id={"row": flipped(row, o)}, device_id_type=MESH,
        )

    def pack(o):
        target = flipped(row, o)
        word = jnp.int32(0)
        scale = jnp.int32(1)
        count = jnp.int32(0)
        for b in range(number):
            hit = assign_ref[b] == target
            word = word + jnp.where(hit, b * scale, 0)
            scale = jnp.where(hit, scale * 16, scale)
            count = count + jnp.where(hit, 1, 0)
        counts = count_in if o == 0 else count_out
        counts[o] = jnp.full((8, 128), count, jnp.int32)
        for k in range(capacity):
            block = lax.shift_right_logical(word, jnp.int32(4 * k)) & 15
            value = tokens_ref[block]
            value = jnp.where(k < count, value, jnp.zeros_like(value))
            if o == 0:
                arrived[pl.ds(k * length, length)] = value
            else:
                packed[pl.ds(((o - 1) * capacity + k) * length, length)] = value

    inputs_in[0].wait()
    direct_two = [o for o in range(1, levels) if o == 1 or o % 2 == 0]
    shard_two(row)[...] = level_two_ref[...].astype(jnp.bfloat16)
    inputs_in[1].wait()
    pack(2)
    inputs_in[2].wait()
    shard_one(col)[...] = level_one_ref[...].astype(jnp.bfloat16)

    pl.semaphore_wait(barrier, levels - 1 + columns - 1)

    far = [(o, p) for o in range(2, levels) for p in range(own_pieces)]
    for o in reversed(direct_two):
        send_two(o).start()
    send_piece(*far[0]).start()
    for o in range(1, columns):
        send_one(o).start()
    send_count(2).start()
    pack(1)
    send_count(1).start()
    for p in range(own_pieces):
        send_piece(1, p).start()
    for o in range(3, levels):
        pack(o)
        send_count(o).start()
    pack(0)
    for load in loads:
        load.start()

    for o in direct_two:
        if o > 1:
            send_two(o).wait_send()
    send_piece(*far[1]).start()
    for o in range(2, levels, 2):
        send_two(o).wait_recv()
        forward_two(o).start()
    for i in range(2, len(far) - 1):
        send_piece(*far[i - 2]).wait_send()
        send_piece(*far[i]).start()

    grad_one[...] = jnp.zeros_like(grad_one)
    grad_two[...] = jnp.zeros_like(grad_two)
    for o in range(1, levels):
        send_count(o).wait_recv()
    for o in range(1, columns):
        send_one(o).wait_recv()
    for o in range(1, levels, 2):
        send_two(o).wait_recv()

    def tile_body(t, carry):
        for i in range(per_tile):
            g = t * per_tile + i
            part = arrived.at[pl.ds(pl.multiple_of(g * piece * length, piece * length), piece * length)]

            @pl.when(g >= own_pieces)
            def _():
                pltpu.make_async_remote_copy(
                    src_ref=part, dst_ref=part,
                    send_sem=piece_send.at[g], recv_sem=piece_recv.at[g],
                    device_id={"row": flipped(row, 1)}, device_id_type=MESH,
                ).wait_recv()

        inputs = arrived[pl.ds(pl.multiple_of(t * tile_rows, tile_rows), tile_rows)].astype(jnp.float32)
        place = lax.broadcasted_iota(jnp.int32, (tile_rows, 1), 0)
        inner = place % length
        slot = t * tile_slots + place // length
        if capacity >= tile_slots:
            count = count_in[(t * tile_slots) // capacity][0:1, 0:1]
        else:
            count = jnp.zeros((1, 1), jnp.int32)
            per_source = tile_slots // capacity
            for i in range(per_source):
                own = count_in[t * per_source + i][0:1, 0:1]
                count = jnp.where(place // (capacity * length) == i, own, count)
        filled = (slot % capacity < count).astype(jnp.float32)
        loss_weight = filled * (inner < length - 1).astype(jnp.float32) * loss_scale
        targets = jnp.where(inner < length - 1, pltpu.roll(inputs, tile_rows - 1, 0), 0.0)

        factor_one = lax.rsqrt(jnp.mean(inputs * inputs, axis=-1, keepdims=True) + norm_eps)
        act_one = (inputs * factor_one).astype(jnp.bfloat16)
        pre_one = shrink * jnp.dot(act_one, weight_one[...], preferred_element_type=jnp.float32)
        gate_one = jax.nn.sigmoid(pre_one)
        hidden = inputs + pre_one * gate_one
        factor_two = lax.rsqrt(jnp.mean(hidden * hidden, axis=-1, keepdims=True) + norm_eps)
        normed_two = hidden * factor_two
        act_two = normed_two.astype(jnp.bfloat16)
        pre_two = shrink * jnp.dot(act_two, weight_two[...], preferred_element_type=jnp.float32)
        gate_two = jax.nn.sigmoid(pre_two)
        grad_out = loss_weight * (hidden + pre_two * gate_two - targets)
        grad_pre_two = (grad_out * (gate_two * (1.0 + pre_two * (1.0 - gate_two)))).astype(jnp.bfloat16)
        grad_two[...] += lax.dot_general(
            act_two, grad_pre_two, (((0,), (0,)), ((), ())), preferred_element_type=jnp.float32
        )
        grad_act = shrink * lax.dot_general(
            grad_pre_two, weight_two[...], (((1,), (1,)), ((), ())),
            preferred_element_type=jnp.float32,
        )
        grad_hidden = grad_out + factor_two * (
            grad_act - normed_two * jnp.mean(grad_act * normed_two, axis=-1, keepdims=True)
        )
        grad_pre_one = (grad_hidden * (gate_one * (1.0 + pre_one * (1.0 - gate_one)))).astype(jnp.bfloat16)
        grad_one[...] += lax.dot_general(
            act_one, grad_pre_one, (((0,), (0,)), ((), ())), preferred_element_type=jnp.float32
        )
        return carry

    first_tiles = max(1, own_pieces // per_tile)
    lax.fori_loop(0, first_tiles, tile_body, 0)
    send_piece(*far[-3]).wait_send()
    send_piece(*far[-1]).start()
    lax.fori_loop(first_tiles, tiles, tile_body, 0)

    for load in loads:
        load.wait()

    def direction(grad, first, second, index, rows):
        at = pl.ds(pl.multiple_of(index * rows, rows), rows)
        return adam_direction(shrink * grad[at, :], first[at, :], second[at, :])

    def send_direction_one(o):
        return pltpu.make_async_remote_copy(
            src_ref=out_one.at[o], dst_ref=in_one.at[o],
            send_sem=d1_send.at[o], recv_sem=d1_recv.at[o],
            device_id={"col": (col + o) % columns}, device_id_type=MESH,
        )

    def send_direction_two(o):
        return pltpu.make_async_remote_copy(
            src_ref=out_two.at[o], dst_ref=in_two.at[o],
            send_sem=d2_send.at[o], recv_sem=d2_recv.at[o],
            device_id={"row": flipped(row, o)}, device_id_type=MESH,
        )

    def relay(target):
        return pltpu.make_async_remote_copy(
            src_ref=relay_out, dst_ref=relay_in, send_sem=relay_send, recv_sem=relay_recv,
            device_id={"col": target}, device_id_type=MESH,
        )

    def one_for(index):
        return direction(grad_one, adam_one_m, adam_one_v, index, rows_one)

    def start_one(o):
        out_one[o] = one_for((col + o) % columns).astype(jnp.bfloat16)
        send_direction_one(o).start()

    def start_two(o):
        out_two[o] = direction(
            grad_two, adam_two_m, adam_two_v, flipped(row, o), rows_two
        ).astype(jnp.bfloat16)
        send_direction_two(o).start()

    line = columns == 4
    if line:
        at_end = lax.rem(col, 3) == 0

        @pl.when(at_end)
        def _():
            relay_out[...] = one_for(3 - col).astype(jnp.bfloat16)

        @pl.when(col == 0)
        def _():
            relay(1).start()
            start_one(2)
            start_one(1)

        @pl.when(col == 3)
        def _():
            relay(2).start()
            start_one(2)
            start_one(3)

        @pl.when(col == 1)
        def _():
            start_one(3)
            start_one(1)

        @pl.when(col == 2)
        def _():
            start_one(1)
            start_one(3)
    else:
        for o in range(1, columns):
            start_one(o)
    for o in range(levels - 1, 0, -1):
        start_two(o)
    if line:
        @pl.when(jnp.logical_not(at_end))
        def _():
            own_one[...] = one_for(3 * (2 - col))
            relay(3 * (2 - col)).wait_recv()
            out_one[2] = (own_one[...] + relay_in[...].astype(jnp.float32)).astype(jnp.bfloat16)
            send_direction_one(2).start()

    own_one[...] = one_for(col)
    own_two[...] = direction(grad_two, adam_two_m, adam_two_v, row, rows_two)

    for o in range(1, levels):
        send_direction_two(o).wait_recv()
    total_two = own_two[...]
    for o in range(1, levels):
        total_two = total_two + in_two[o].astype(jnp.float32)
    mean_two_ref[...] = total_two / levels

    def receive_one(sent, offsets):
        for o in offsets:
            send_direction_one(o).wait_recv()
        total_one = own_one[...]
        for o in offsets:
            total_one = total_one + in_one[o].astype(jnp.float32)
        mean_one_ref[...] = total_one / columns
        for o in sent:
            send_direction_one(o).wait_send()

    if line:
        @pl.when(col == 0)
        def _():
            receive_one((1, 2), (3, 2))
            relay(1).wait_send()

        @pl.when(col == 3)
        def _():
            receive_one((2, 3), (1, 2))
            relay(2).wait_send()

        @pl.when(jnp.logical_not(at_end))
        def _():
            receive_one((1, 2, 3), (1, 3, 2))
    else:
        receive_one(range(1, columns), range(1, columns))

    for o in range(1, columns):
        send_one(o).wait_send()
    send_two(1).wait_send()
    for o in range(2, levels, 2):
        forward_two(o).wait_send()
    for o in range(1, levels):
        send_count(o).wait_send()
        send_direction_two(o).wait_send()
        for p in range(own_pieces):
            if o == 1 or (o, p) in far[-2:]:
                send_piece(o, p).wait_send()


def per_device(
    tokens, assign, level_one, moment_one, level_two, moment_two,
    first_one, second_one, first_two, second_two,
):
    levels = lax.axis_size("row")
    columns = lax.axis_size("col")
    blocks = tokens[0, 0]
    number, length, features = blocks.shape
    capacity = max(2, (2 * number + levels - 1) // levels)
    rows_one = features // columns
    rows_two = features // levels
    piece = min(capacity, tile_slots)
    pieces = levels * capacity // piece
    f32, bf16 = jnp.float32, jnp.bfloat16
    vmem = pl.BlockSpec(memory_space=pltpu.VMEM)
    smem = pl.BlockSpec(memory_space=pltpu.SMEM)
    hbm = pl.BlockSpec(memory_space=pltpu.HBM)
    dma = pltpu.SemaphoreType.DMA
    square = (features, features)
    mean_one, mean_two = pl.pallas_call(
        functools.partial(kernel, levels, columns, capacity),
        out_shape=[
            jax.ShapeDtypeStruct((rows_one, features), f32),
            jax.ShapeDtypeStruct((rows_two, features), f32),
        ],
        in_specs=[smem] + [hbm] * 7,
        out_specs=[vmem] * 2,
        scratch_shapes=[
            pltpu.VMEM((number, length, features), bf16),
            pltpu.VMEM((rows_one, features), f32),
            pltpu.VMEM((rows_two, features), f32),
            pltpu.VMEM((rows_one, features), bf16),
            pltpu.VMEM((rows_one, features), bf16),
            pltpu.VMEM(((levels - 1) * capacity * length, features), bf16),
            pltpu.VMEM((levels * capacity * length, features), bf16),
            pltpu.VMEM((levels, 8, 128), jnp.int32),
            pltpu.VMEM((levels, 8, 128), jnp.int32),
            pltpu.VMEM(square, bf16),
            pltpu.VMEM(square, bf16),
            pltpu.VMEM(square, f32),
            pltpu.VMEM(square, f32),
            pltpu.VMEM(square, f32),
            pltpu.VMEM(square, f32),
            pltpu.VMEM(square, f32),
            pltpu.VMEM(square, f32),
            pltpu.VMEM((rows_one, features), f32),
            pltpu.VMEM((rows_two, features), f32),
            pltpu.VMEM((columns, rows_one, features), bf16),
            pltpu.VMEM((levels, rows_two, features), bf16),
            pltpu.VMEM((columns, rows_one, features), bf16),
            pltpu.VMEM((levels, rows_two, features), bf16),
            dma((7,)),
            dma((pieces,)), dma((pieces,)),
            dma((levels,)), dma((levels,)),
            dma((columns,)), dma((columns,)),
            dma((levels,)), dma((levels,)), dma((levels,)),
            dma((columns,)), dma((columns,)),
            dma((levels,)), dma((levels,)),
            dma, dma,
        ],
        compiler_params=pltpu.CompilerParams(
            collective_id=0, has_side_effects=True, vmem_limit_bytes=56 * 1024 * 1024
        ),
        name="outer_round",
    )(
        assign.reshape(number), blocks, level_one[0], level_two[0],
        first_one[0, 0], second_one[0, 0], first_two[0, 0], second_two[0, 0],
    )
    new_one, new_moment_one = outer_update(level_one[0], moment_one[0], mean_one)
    new_two, new_moment_two = outer_update(level_two[0], moment_two[0], mean_two)
    return (new_one[None], new_moment_one[None], new_two[None], new_moment_two[None])


def solution(mesh):
    in_specs = (
        P(("groups", "row"), "col", None, None, None),
        P(("groups", "row"), "col", None, None),
        P(("groups", "row"), "col", None),
        P(("groups", "row"), "col", None),
        P(("groups", "col"), "row", None),
        P(("groups", "col"), "row", None),
        P(("groups", "row"), "col", None, None),
        P(("groups", "row"), "col", None, None),
        P(("groups", "row"), "col", None, None),
        P(("groups", "row"), "col", None, None),
    )
    out_specs = (
        P(("groups", "row"), "col", None),
        P(("groups", "row"), "col", None),
        P(("groups", "col"), "row", None),
        P(("groups", "col"), "row", None),
    )
    return jax.shard_map(
        per_device, mesh=mesh, in_specs=in_specs, out_specs=out_specs, check_vma=False
    )
```

```python
import functools

import jax
import jax.numpy as jnp
from jax import lax
from jax.experimental import pallas as pl
from jax.experimental.pallas import tpu as pltpu
from jax.sharding import PartitionSpec as P

norm_eps = 1e-06
adam_eps = 1e-08
beta_first = 0.9
beta_second = 0.95
bias_first = 0.19
bias_second = 0.0975
inner_rate = 0.3
decay_rate = 0.1
outer_rate = 0.7
momentum = 0.9

tile_slots = 8
MESH = pl.DeviceIdType.MESH


def flipped(index, mask):
    bit = 1
    while bit <= mask:
        if mask & bit:
            index = index + bit * (1 - 2 * (lax.div(index, bit) % 2))
        bit *= 2
    return index


def outer_update(weight, moment, mean_direction):
    pseudo = inner_rate * (mean_direction + decay_rate * weight)
    moment_new = momentum * moment + pseudo
    return weight - outer_rate * (pseudo + momentum * moment_new), moment_new


def adam_direction(gradient, first_moment, second_moment):
    first_new = beta_first * first_moment + (1.0 - beta_first) * gradient
    second_new = beta_second * second_moment + (1.0 - beta_second) * gradient * gradient
    return (first_new * (1.0 / bias_first)) / (
        jnp.sqrt(second_new * (1.0 / bias_second)) + adam_eps
    )


def kernel(
    levels, columns, capacity,
    assign_ref, tokens_hbm, level_one_hbm, level_two_hbm,
    first_one_ref, second_one_ref, first_two_ref, second_two_ref,
    mean_one_ref, mean_two_ref,
    tokens_ref, level_one_ref, level_two_ref, relay_in, relay_out, packed, arrived, count_out, count_in, weight_one, weight_two,
    adam_one_m, adam_one_v, adam_two_m, adam_two_v, grad_one, grad_two,
    own_one, own_two, out_one, out_two, in_one, in_two,
    local_sem, piece_send, piece_recv, count_send, count_recv,
    w1_send, w1_recv, w2_send, w2_forward, w2_recv, d1_send, d1_recv, d2_send, d2_recv,
    relay_send, relay_recv,
):
    row = lax.axis_index("row")
    col = lax.axis_index("col")
    number, length, features = tokens_ref.shape
    rows_one = features // columns
    rows_two = features // levels
    piece = min(capacity, tile_slots)
    own_pieces = capacity // piece
    per_tile = tile_slots // piece
    tiles = levels * capacity // tile_slots
    tile_rows = tile_slots * length
    shrink = features ** (-0.5)
    loss_scale = 1.0 / (number * length)

    barrier = pltpu.get_barrier_semaphore()
    for o in range(1, levels):
        pl.semaphore_signal(
            barrier, inc=1, device_id={"row": flipped(row, o)}, device_id_type=MESH
        )
    for o in range(1, columns):
        pl.semaphore_signal(
            barrier, inc=1, device_id={"col": (col + o) % columns}, device_id_type=MESH
        )

    loads = [
        pltpu.make_async_copy(source, target, local_sem.at[i])
        for i, (source, target) in enumerate((
            (first_one_ref, adam_one_m), (second_one_ref, adam_one_v),
            (first_two_ref, adam_two_m), (second_two_ref, adam_two_v),
        ))
    ]
    inputs_in = [
        pltpu.make_async_copy(source, target, local_sem.at[4 + i])
        for i, (source, target) in enumerate((
            (level_two_hbm, level_two_ref), (tokens_hbm, tokens_ref), (level_one_hbm, level_one_ref),
        ))
    ]
    for load in inputs_in:
        load.start()

    def shard_one(index):
        return weight_one.at[pl.ds(pl.multiple_of(index * rows_one, rows_one), rows_one)]

    def shard_two(index):
        return weight_two.at[pl.ds(pl.multiple_of(index * rows_two, rows_two), rows_two)]

    def send_one(o):
        return pltpu.make_async_remote_copy(
            src_ref=shard_one(col), dst_ref=shard_one(col),
            send_sem=w1_send.at[o], recv_sem=w1_recv.at[o],
            device_id={"col": (col + o) % columns}, device_id_type=MESH,
        )

    def send_two(o):
        return pltpu.make_async_remote_copy(
            src_ref=shard_two(row), dst_ref=shard_two(row),
            send_sem=w2_send.at[o], recv_sem=w2_recv.at[o],
            device_id={"row": flipped(row, o)}, device_id_type=MESH,
        )

    def forward_two(o):
        source = flipped(row, o)
        return pltpu.make_async_remote_copy(
            src_ref=shard_two(source), dst_ref=shard_two(source),
            send_sem=w2_forward.at[o], recv_sem=w2_recv.at[o + 1],
            device_id={"row": flipped(row, 1)}, device_id_type=MESH,
        )

    direct_two = [o for o in range(1, levels) if o == 1 or o % 2 == 0]
    def send_piece(o, p):
        start = (o - 1) * capacity + p * piece
        return pltpu.make_async_remote_copy(
            src_ref=packed.at[pl.ds(start * length, piece * length)],
            dst_ref=arrived.at[pl.ds((start + capacity) * length, piece * length)],
            send_sem=piece_send.at[o * own_pieces + p],
            recv_sem=piece_recv.at[o * own_pieces + p],
            device_id={"row": flipped(row, o)}, device_id_type=MESH,
        )

    def send_count(o):
        return pltpu.make_async_remote_copy(
            src_ref=count_out.at[o], dst_ref=count_in.at[o],
            send_sem=count_send.at[o], recv_sem=count_recv.at[o],
            device_id={"row": flipped(row, o)}, device_id_type=MESH,
        )

    def pack(o):
        target = flipped(row, o)
        word = jnp.int32(0)
        scale = jnp.int32(1)
        count = jnp.int32(0)
        for b in range(number):
            hit = assign_ref[b] == target
            word = word + jnp.where(hit, b * scale, 0)
            scale = jnp.where(hit, scale * 16, scale)
            count = count + jnp.where(hit, 1, 0)
        counts = count_in if o == 0 else count_out
        counts[o] = jnp.full((8, 128), count, jnp.int32)
        for k in range(capacity):
            block = lax.shift_right_logical(word, jnp.int32(4 * k)) & 15
            value = tokens_ref[block]
            value = jnp.where(k < count, value, jnp.zeros_like(value))
            if o == 0:
                arrived[pl.ds(k * length, length)] = value
            else:
                packed[pl.ds(((o - 1) * capacity + k) * length, length)] = value

    inputs_in[0].wait()
    direct_two = [o for o in range(1, levels) if o == 1 or o % 2 == 0]
    shard_two(row)[...] = level_two_ref[...].astype(jnp.bfloat16)
    inputs_in[1].wait()
    pack(2)
    inputs_in[2].wait()
    shard_one(col)[...] = level_one_ref[...].astype(jnp.bfloat16)

    pl.semaphore_wait(barrier, levels - 1 + columns - 1)

    for o in reversed(direct_two):
        send_two(o).start()
    for p in range(own_pieces):
        send_piece(2, p).start()
    for o in range(1, columns):
        send_one(o).start()
    send_count(2).start()
    pack(1)
    send_count(1).start()
    for p in range(own_pieces):
        send_piece(1, p).start()
    for o in range(3, levels):
        pack(o)
        send_count(o).start()
        for p in range(own_pieces):
            send_piece(o, p).start()
    pack(0)
    for load in loads:
        load.start()

    for o in direct_two:
        if o > 1:
            send_two(o).wait_send()
    for o in range(2, levels, 2):
        send_two(o).wait_recv()
        forward_two(o).start()

    grad_one[...] = jnp.zeros_like(grad_one)
    grad_two[...] = jnp.zeros_like(grad_two)
    for o in range(1, levels):
        send_count(o).wait_recv()
    for o in range(1, columns):
        send_one(o).wait_recv()
    for o in range(1, levels, 2):
        send_two(o).wait_recv()

    def tile_body(t, carry):
        for i in range(per_tile):
            g = t * per_tile + i
            part = arrived.at[pl.ds(pl.multiple_of(g * piece * length, piece * length), piece * length)]

            @pl.when(g >= own_pieces)
            def _():
                pltpu.make_async_remote_copy(
                    src_ref=part, dst_ref=part,
                    send_sem=piece_send.at[g], recv_sem=piece_recv.at[g],
                    device_id={"row": flipped(row, 1)}, device_id_type=MESH,
                ).wait_recv()

        inputs = arrived[pl.ds(pl.multiple_of(t * tile_rows, tile_rows), tile_rows)].astype(jnp.float32)
        place = lax.broadcasted_iota(jnp.int32, (tile_rows, 1), 0)
        inner = place % length
        slot = t * tile_slots + place // length
        if capacity >= tile_slots:
            count = count_in[(t * tile_slots) // capacity][0:1, 0:1]
        else:
            count = jnp.zeros((1, 1), jnp.int32)
            per_source = tile_slots // capacity
            for i in range(per_source):
                own = count_in[t * per_source + i][0:1, 0:1]
                count = jnp.where(place // (capacity * length) == i, own, count)
        filled = (slot % capacity < count).astype(jnp.float32)
        loss_weight = filled * (inner < length - 1).astype(jnp.float32) * loss_scale
        targets = jnp.where(inner < length - 1, pltpu.roll(inputs, tile_rows - 1, 0), 0.0)

        factor_one = lax.rsqrt(jnp.mean(inputs * inputs, axis=-1, keepdims=True) + norm_eps)
        act_one = (inputs * factor_one).astype(jnp.bfloat16)
        pre_one = shrink * jnp.dot(act_one, weight_one[...], preferred_element_type=jnp.float32)
        gate_one = jax.nn.sigmoid(pre_one)
        hidden = inputs + pre_one * gate_one
        factor_two = lax.rsqrt(jnp.mean(hidden * hidden, axis=-1, keepdims=True) + norm_eps)
        normed_two = hidden * factor_two
        act_two = normed_two.astype(jnp.bfloat16)
        pre_two = shrink * jnp.dot(act_two, weight_two[...], preferred_element_type=jnp.float32)
        gate_two = jax.nn.sigmoid(pre_two)
        grad_out = loss_weight * (hidden + pre_two * gate_two - targets)
        grad_pre_two = (grad_out * (gate_two * (1.0 + pre_two * (1.0 - gate_two)))).astype(jnp.bfloat16)
        grad_two[...] += lax.dot_general(
            act_two, grad_pre_two, (((0,), (0,)), ((), ())), preferred_element_type=jnp.float32
        )
        grad_act = shrink * lax.dot_general(
            grad_pre_two, weight_two[...], (((1,), (1,)), ((), ())),
            preferred_element_type=jnp.float32,
        )
        grad_hidden = grad_out + factor_two * (
            grad_act - normed_two * jnp.mean(grad_act * normed_two, axis=-1, keepdims=True)
        )
        grad_pre_one = (grad_hidden * (gate_one * (1.0 + pre_one * (1.0 - gate_one)))).astype(jnp.bfloat16)
        grad_one[...] += lax.dot_general(
            act_one, grad_pre_one, (((0,), (0,)), ((), ())), preferred_element_type=jnp.float32
        )
        return carry

    lax.fori_loop(0, tiles, tile_body, 0)

    for load in loads:
        load.wait()

    def direction(grad, first, second, index, rows):
        at = pl.ds(pl.multiple_of(index * rows, rows), rows)
        return adam_direction(shrink * grad[at, :], first[at, :], second[at, :])

    def send_direction_one(o):
        return pltpu.make_async_remote_copy(
            src_ref=out_one.at[o], dst_ref=in_one.at[o],
            send_sem=d1_send.at[o], recv_sem=d1_recv.at[o],
            device_id={"col": (col + o) % columns}, device_id_type=MESH,
        )

    def send_direction_two(o):
        return pltpu.make_async_remote_copy(
            src_ref=out_two.at[o], dst_ref=in_two.at[o],
            send_sem=d2_send.at[o], recv_sem=d2_recv.at[o],
            device_id={"row": flipped(row, o)}, device_id_type=MESH,
        )

    def relay(target):
        return pltpu.make_async_remote_copy(
            src_ref=relay_out, dst_ref=relay_in, send_sem=relay_send, recv_sem=relay_recv,
            device_id={"col": target}, device_id_type=MESH,
        )

    def one_for(index):
        return direction(grad_one, adam_one_m, adam_one_v, index, rows_one)

    def start_one(o):
        out_one[o] = one_for((col + o) % columns).astype(jnp.bfloat16)
        send_direction_one(o).start()

    def start_two(o):
        out_two[o] = direction(
            grad_two, adam_two_m, adam_two_v, flipped(row, o), rows_two
        ).astype(jnp.bfloat16)
        send_direction_two(o).start()

    line = columns == 4
    if line:
        at_end = lax.rem(col, 3) == 0

        @pl.when(at_end)
        def _():
            relay_out[...] = one_for(3 - col).astype(jnp.bfloat16)

        @pl.when(col == 0)
        def _():
            relay(1).start()
            start_one(2)
            start_one(1)

        @pl.when(col == 3)
        def _():
            relay(2).start()
            start_one(2)
            start_one(3)

        @pl.when(col == 1)
        def _():
            start_one(3)
            start_one(1)

        @pl.when(col == 2)
        def _():
            start_one(1)
            start_one(3)
    else:
        for o in range(1, columns):
            start_one(o)
    for o in range(levels - 1, 0, -1):
        start_two(o)
    if line:
        @pl.when(jnp.logical_not(at_end))
        def _():
            own_one[...] = one_for(3 * (2 - col))
            relay(3 * (2 - col)).wait_recv()
            out_one[2] = (own_one[...] + relay_in[...].astype(jnp.float32)).astype(jnp.bfloat16)
            send_direction_one(2).start()

    own_one[...] = one_for(col)
    own_two[...] = direction(grad_two, adam_two_m, adam_two_v, row, rows_two)

    for o in range(1, levels):
        send_direction_two(o).wait_recv()
    total_two = own_two[...]
    for o in range(1, levels):
        total_two = total_two + in_two[o].astype(jnp.float32)
    mean_two_ref[...] = total_two / levels

    def receive_one(sent, offsets):
        for o in offsets:
            send_direction_one(o).wait_recv()
        total_one = own_one[...]
        for o in offsets:
            total_one = total_one + in_one[o].astype(jnp.float32)
        mean_one_ref[...] = total_one / columns
        for o in sent:
            send_direction_one(o).wait_send()

    if line:
        @pl.when(col == 0)
        def _():
            receive_one((1, 2), (3, 2))
            relay(1).wait_send()

        @pl.when(col == 3)
        def _():
            receive_one((2, 3), (1, 2))
            relay(2).wait_send()

        @pl.when(jnp.logical_not(at_end))
        def _():
            receive_one((1, 2, 3), (1, 3, 2))
    else:
        receive_one(range(1, columns), range(1, columns))

    for o in range(1, columns):
        send_one(o).wait_send()
    send_two(1).wait_send()
    for o in range(2, levels, 2):
        forward_two(o).wait_send()
    for o in range(1, levels):
        send_count(o).wait_send()
        send_direction_two(o).wait_send()
        for p in range(own_pieces):
            send_piece(o, p).wait_send()


def per_device(
    tokens, assign, level_one, moment_one, level_two, moment_two,
    first_one, second_one, first_two, second_two,
):
    levels = lax.axis_size("row")
    columns = lax.axis_size("col")
    blocks = tokens[0, 0]
    number, length, features = blocks.shape
    capacity = max(2, (2 * number + levels - 1) // levels)
    rows_one = features // columns
    rows_two = features // levels
    piece = min(capacity, tile_slots)
    pieces = levels * capacity // piece
    f32, bf16 = jnp.float32, jnp.bfloat16
    vmem = pl.BlockSpec(memory_space=pltpu.VMEM)
    smem = pl.BlockSpec(memory_space=pltpu.SMEM)
    hbm = pl.BlockSpec(memory_space=pltpu.HBM)
    dma = pltpu.SemaphoreType.DMA
    square = (features, features)
    mean_one, mean_two = pl.pallas_call(
        functools.partial(kernel, levels, columns, capacity),
        out_shape=[
            jax.ShapeDtypeStruct((rows_one, features), f32),
            jax.ShapeDtypeStruct((rows_two, features), f32),
        ],
        in_specs=[smem] + [hbm] * 7,
        out_specs=[vmem] * 2,
        scratch_shapes=[
            pltpu.VMEM((number, length, features), bf16),
            pltpu.VMEM((rows_one, features), f32),
            pltpu.VMEM((rows_two, features), f32),
            pltpu.VMEM((rows_one, features), bf16),
            pltpu.VMEM((rows_one, features), bf16),
            pltpu.VMEM(((levels - 1) * capacity * length, features), bf16),
            pltpu.VMEM((levels * capacity * length, features), bf16),
            pltpu.VMEM((levels, 8, 128), jnp.int32),
            pltpu.VMEM((levels, 8, 128), jnp.int32),
            pltpu.VMEM(square, bf16),
            pltpu.VMEM(square, bf16),
            pltpu.VMEM(square, f32),
            pltpu.VMEM(square, f32),
            pltpu.VMEM(square, f32),
            pltpu.VMEM(square, f32),
            pltpu.VMEM(square, f32),
            pltpu.VMEM(square, f32),
            pltpu.VMEM((rows_one, features), f32),
            pltpu.VMEM((rows_two, features), f32),
            pltpu.VMEM((columns, rows_one, features), bf16),
            pltpu.VMEM((levels, rows_two, features), bf16),
            pltpu.VMEM((columns, rows_one, features), bf16),
            pltpu.VMEM((levels, rows_two, features), bf16),
            dma((7,)),
            dma((pieces,)), dma((pieces,)),
            dma((levels,)), dma((levels,)),
            dma((columns,)), dma((columns,)),
            dma((levels,)), dma((levels,)), dma((levels,)),
            dma((columns,)), dma((columns,)),
            dma((levels,)), dma((levels,)),
            dma, dma,
        ],
        compiler_params=pltpu.CompilerParams(
            collective_id=0, has_side_effects=True, vmem_limit_bytes=56 * 1024 * 1024
        ),
        name="outer_round",
    )(
        assign.reshape(number), blocks, level_one[0], level_two[0],
        first_one[0, 0], second_one[0, 0], first_two[0, 0], second_two[0, 0],
    )
    new_one, new_moment_one = outer_update(level_one[0], moment_one[0], mean_one)
    new_two, new_moment_two = outer_update(level_two[0], moment_two[0], mean_two)
    return (new_one[None], new_moment_one[None], new_two[None], new_moment_two[None])


def solution(mesh):
    in_specs = (
        P(("groups", "row"), "col", None, None, None),
        P(("groups", "row"), "col", None, None),
        P(("groups", "row"), "col", None),
        P(("groups", "row"), "col", None),
        P(("groups", "col"), "row", None),
        P(("groups", "col"), "row", None),
        P(("groups", "row"), "col", None, None),
        P(("groups", "row"), "col", None, None),
        P(("groups", "row"), "col", None, None),
        P(("groups", "row"), "col", None, None),
    )
    out_specs = (
        P(("groups", "row"), "col", None),
        P(("groups", "row"), "col", None),
        P(("groups", "col"), "row", None),
        P(("groups", "col"), "row", None),
    )
    return jax.shard_map(
        per_device, mesh=mesh, in_specs=in_specs, out_specs=out_specs, check_vma=False
    )
```
